32 devices in a mesh: groups: 2 (over y), blk: 8 (over z, x), sub: 2 (over core).
Axes of the slice: x: 2, y: 2, z: 4, core: 2. Of those that a mesh axis runs over, the one named last changes fastest.
Arguments:
- embeddings: bfloat16 [32, 1024, 384], P(('groups', 'blk', 'sub')), parts along dimension 0, may hold values from -0.3046875 to 0.3046875
- local_scales: bfloat16 [32, 1024], P(('groups', 'blk', 'sub')), parts along dimension 0, may hold values from 0.796875 to 2.5
- start: bfloat16 [32, 1024, 64], P(('groups', 'blk', 'sub')), parts along dimension 0, may hold values from -6 to 6
- pairs: int32 [64, 2], P('groups'), parts along dimension 0, may hold values from 0 to 15, as said below
Outputs:
- basis: float32 [32, 1024, 64], P(('groups', 'blk', 'sub')), parts along dimension 0
The draws below stay inside these ranges and needn't reach their ends.
There are 2 independent parts, one for each index of `groups`. The reference program is written for one: setup_inputs(seed, part) draws one part's arguments, and reference() takes and returns one part's arrays. A program takes and returns all parts, laid end to end along the dimension named above; each array names one. Nothing has to cross between parts.
Inputs may be any that keep to these rules, and one draw needn't show every extreme that they name: Block b lies on device b. Every pair has row block <= column block, and the column block's device index exceeds the row block's by 0 to 4. Pairs may repeat and stand in any order. The pairs whose row block lies on one device number 0 to 4, and some device has exactly 4.
All inputs are finite; a program needn't handle non-finite values.
Results may differ from the reference program's by a relative error of at most 0.0036.
Values may be sent and summed in bfloat16 or wider, within the bound.
A program may use at most 64 MiB of HBM per device.

```python
import math
import jax
import jax.numpy as jnp
from jax import lax

D = 384
K = 64
BLOCK = 1024
BLK_DEV = 1
REACH = 4
NBLOCKS = 16
PAIRS = 32
ROWS = 16384


def draw_pairs(key, part):
    key = jax.random.fold_in(key, 11)
    keys = jax.random.split(key, 6)
    devices = NBLOCKS // BLK_DEV
    average = 2 * BLK_DEV
    extra = jax.random.randint(keys[0], (devices // 2,), 0, average + 1).at[0].set(average)
    paired = jnp.concatenate([average + extra, average - extra]).astype(jnp.int32)
    order = jax.random.permutation(keys[1], devices)
    counts = jnp.zeros((devices,), jnp.int32).at[order].set(paired)
    ends = jnp.cumsum(counts).astype(jnp.int32)
    position = jnp.arange(PAIRS, dtype=jnp.int32)
    owner = jnp.sum((ends[None, :] <= position[:, None]).astype(jnp.int32), 1)
    distance = jax.random.randint(keys[2], (PAIRS,), 0, REACH + 1)
    distance = jnp.where(position <= REACH, position, distance)
    col_dev = jnp.minimum(owner + distance, devices - 1)
    first = owner * BLK_DEV + jax.random.randint(keys[3], (PAIRS,), 0, BLK_DEV)
    second = col_dev * BLK_DEV + jax.random.randint(keys[4], (PAIRS,), 0, BLK_DEV)
    row_blk = jnp.minimum(first, second)
    col_blk = jnp.maximum(first, second)
    stacked = jnp.stack([row_blk, col_blk], 1).astype(jnp.int32)
    shuffle = jax.random.permutation(keys[5], PAIRS)
    return stacked[shuffle]


def level_of(rng, dims, pieces, least, top_value):
    loudness = 1.0
    for axis_at, parts in pieces:
        steps = jax.random.uniform(jax.random.fold_in(jax.random.fold_in(rng, 6), axis_at), (parts,), jnp.float32, least / len(pieces), top_value / len(pieces))
        loudness = loudness * jnp.repeat(jnp.exp(steps), dims[axis_at] // parts).reshape((-1,) + (1,) * (len(dims) - 1 - axis_at))
    return loudness


def centred(key, dims, scale, bound, shards=(), held_as=jnp.bfloat16):
    result = scale * jax.random.normal(key, dims, jnp.float32)
    if shards:
        result = result * level_of(key, dims, shards, -0.22, 0.18)
    return jnp.clip(result, -bound, bound).astype(held_as)


def setup_inputs(seed: int = 0, part: int = 0) -> dict:
    seeds = jax.random.split(jax.random.key(seed), 5)
    own_keys = jax.random.split(jax.random.fold_in(seeds[4], part), 5)
    return {
        "embeddings": centred(own_keys[0], (NBLOCKS, BLOCK, D), (D ** -0.5), 0.3046875, ((0, 16),)),
        "local_scales": jnp.clip(jnp.exp(math.log(2.5) - 1.1433482 * jax.random.uniform(own_keys[1], (NBLOCKS, BLOCK), jnp.float32) ** level_of(own_keys[1], (NBLOCKS, BLOCK), ((0, 16),), -0.2, 0.2)), 0.796875, 2.5).astype(jnp.bfloat16),
        "start": centred(own_keys[2], (NBLOCKS, BLOCK, K), 1.0, 6.0, ((0, 16),)),
        "pairs": draw_pairs(jax.random.fold_in(jax.random.fold_in(seeds[4], part), 71), part),
    }


def affinity(left, right, left_scale, right_scale):
    left_f = left.astype(jnp.float32)
    right_f = right.astype(jnp.float32)
    cross = jnp.dot(left_f, right_f.T, precision=lax.Precision.HIGHEST)
    left_sq = lax.optimization_barrier(jnp.sum(left_f * left_f, -1))
    right_sq = lax.optimization_barrier(jnp.sum(right_f * right_f, -1))
    dist = left_sq[:, None] + right_sq[None, :] - 2.0 * cross
    scale = left_scale.astype(jnp.float32)[:, None] * right_scale.astype(jnp.float32)[None, :]
    return jnp.exp(-dist / scale).astype(jnp.bfloat16)

def product(embeddings, local_scales, vectors, pairs):

    def step(total, pair):
        row_blk = pair[0]
        col_blk = pair[1]
        tile_f = affinity(embeddings[row_blk], embeddings[col_blk], local_scales[row_blk], local_scales[col_blk]).astype(jnp.float32)
        toward_row = jnp.dot(tile_f, vectors[col_blk].astype(jnp.float32), precision=lax.Precision.HIGHEST)
        toward_col = jnp.dot(tile_f.T, vectors[row_blk].astype(jnp.float32), precision=lax.Precision.HIGHEST)
        total = total.at[row_blk].add(toward_row)
        total = total.at[col_blk].add(toward_col)
        return (total, None)
    empty = jnp.zeros(vectors.shape, jnp.float32)
    return lax.scan(step, empty, pairs)[0]

def orthonormal(values):
    flat = values.reshape(-1, values.shape[-1])
    gram_sum = jnp.dot(flat.T, flat, precision=lax.Precision.HIGHEST)
    lower = jnp.linalg.cholesky(gram_sum)
    solved = lax.linalg.triangular_solve(lower, flat, left_side=False, lower=True, transpose_a=True)
    return solved.reshape(values.shape)

def reference(embeddings, local_scales, start, pairs):
    first = product(embeddings, local_scales, start, pairs)
    q_first = orthonormal(first).astype(jnp.bfloat16)
    second = product(embeddings, local_scales, q_first, pairs)
    return math.sqrt(ROWS) * orthonormal(second)
```

```python
import functools
import math

import jax
import jax.numpy as jnp
from jax import lax
from jax.experimental import pallas as pl
from jax.experimental.pallas import tpu as pltpu
from jax.sharding import PartitionSpec as P

REACH = 4
CHUNKS = 4
STEP = 4
MESH = pl.DeviceIdType.MESH
HIGH = lax.Precision.HIGHEST
F32 = jnp.float32
BF16 = jnp.bfloat16
NN = (((1,), (0,)), ((), ()))
NT = (((1,), (1,)), ((), ()))


def inverse_factor(gram):
    size = gram.shape[0]
    eye = (
        lax.broadcasted_iota(jnp.int32, (size, size), 0)
        == lax.broadcasted_iota(jnp.int32, (size, size), 1)
    ).astype(F32)
    both = jnp.concatenate([gram, eye], 1)
    groups = [both[8 * g : 8 * g + 8] for g in range(size // 8)]
    below = lax.broadcasted_iota(jnp.int32, (8, 1), 0)
    done = []
    for j in range(0, size, STEP):
        g, r = divmod(j, 8)
        last = size // 8
        line = [groups[g][r + t : r + t + 1] for t in range(STEP)]
        head = [[line[t][:, j + u : j + u + 1] for u in range(STEP)] for t in range(STEP)]
        cols = [[groups[h][:, j + t : j + t + 1] for h in range(g, last)] for t in range(STEP)]
        inv = []
        for t in range(STEP):
            inv.append(1.0 / head[t][t])
            for u in range(t + 1, STEP):
                f = head[t][u] * inv[t]
                line[u] = line[u] - f * line[t]
                cols[u] = [cu - f * ct for cu, ct in zip(cols[u], cols[t])]
                head[u] = [hu - f * ht for hu, ht in zip(head[u], head[t])]
            done.append(line[t] * lax.rsqrt(head[t][t]))
        scaled = [line[t] * inv[t] for t in range(STEP)]
        for h in range(g, last):
            if h == g and r + STEP == 8:
                continue
            update = cols[0][h - g] * scaled[0]
            for t in range(1, STEP):
                update = update + cols[t][h - g] * scaled[t]
            if h == g:
                update = jnp.where(below >= r + STEP, update, 0.0)
            groups[h] = groups[h] - update
    return jnp.concatenate(done, 0)[:, size:]


def kernel(
    n, rows, width, k, stages, out_scale,
    pairs, scales, start_vec, emb, out,
    pack, col_aux,
    gemb, gpack, qown, gq, tiles, acc, part, got, gram, rowaux,
    mate, msend, mrecv, esend, erecv, qsend, qrecv, psend, precv, gsend, grecv,
):
    i = lax.axis_index(("blk", "sub"))
    core = lax.rem(i, 2)
    quad = lax.rem(i, 4)
    cw = rows // CHUNKS

    def to(dev):
        return {"blk": lax.div(dev, 2), "sub": lax.rem(dev, 2)}

    def remote(src, dst, ss, rs, dev):
        return pltpu.make_async_remote_copy(
            src_ref=src, dst_ref=dst, send_sem=ss, recv_sem=rs, device_id=to(dev), device_id_type=MESH
        )

    barrier = pltpu.get_barrier_semaphore()

    @pl.loop(1, n)
    def _(t):
        pl.semaphore_signal(barrier, inc=1, device_id=to(lax.rem(i + t, n)), device_id_type=MESH)

    pl.semaphore_wait(barrier, n - 1)

    def piece(slot, q):
        if q == 0:
            return pack if slot is None else gpack.at[slot]
        sl = pl.ds((q - 1) * cw, cw)
        return emb.at[sl] if slot is None else gemb.at[slot, sl]

    def send(kind, q, source, slot, dev):
        return remote(piece(source, q), piece(slot, q), esend.at[kind, q], erecv.at[slot, q], dev)

    def wait_piece(slot, q):
        remote(piece(slot, q), piece(slot, q), esend.at[0, q], erecv.at[slot, q], i).wait_recv()

    first_quad, later = quad < 2, quad >= 2
    one, zero = core == 1, core == 0
    own_sends = [
        (0, None, 3, i - 4, i >= 4),
        (1, None, 1, i - 2, later),
        (2, None, 0, i - 1, one),
    ]
    fwd4 = [
        (3, 3, 1, i + 2, first_quad & (i + 4 < n)),
        (5, 3, 2, i + 1, zero & (i + 4 < n)),
    ]
    fwd2 = [
        (4, 1, 2, i - 1, one & (i + 2 < n)),
        (6, 1, 0, i + 1, zero & (i + 2 < n)),
    ]

    def start(entries, q):
        for kind, source, slot, dev, cond in entries:
            @pl.when(cond)
            def _():
                send(kind, q, source, slot, dev).start()

    for q in range(1, CHUNKS + 1):
        start(own_sends, q)
        if q > 1:
            continue
        ones = jnp.ones((8, width), BF16)
        squares = []
        for c in range(CHUNKS):
            x = emb[c * cw : (c + 1) * cw, :].astype(F32)
            x = x * x
            big = x.astype(BF16)
            small = (x - big.astype(F32)).astype(BF16)
            squares.append(
                lax.dot_general(ones, big, NT, preferred_element_type=F32)
                + lax.dot_general(ones, small, NT, preferred_element_type=F32)
            )
        sq = jnp.concatenate(squares, 1)
        scale = scales[...].astype(F32)
        high = sq.astype(BF16).astype(F32)
        mid = (sq - high).astype(BF16).astype(F32)
        low = (sq - high) - mid
        line = lax.broadcasted_iota(jnp.int32, (8, rows), 0)
        tail = jnp.where(line == 0, high, jnp.where(line == 1, mid, jnp.where(line == 2, low, scale)))
        pack[k : k + 16, :] = jnp.concatenate([tail, tail], 0).astype(BF16)
        pack[0:k, :] = start_vec[...].astype(F32).T.astype(BF16)
        col_aux[...] = jnp.where(line == 0, 0.5 * sq, (2.0 / math.log(2.0)) / scale).T
        start(own_sends, 0)

    offset = pairs[:, 1:2] - i
    held = pairs[:, 0:1] == i
    m_ref = [
        jnp.sum((held & (offset == d)).astype(F32), 0, keepdims=True) for d in range(REACH + 1)
    ]

    def prepare_aux(slot):
        tail = (pack if slot is None else gpack.at[slot])[k : k + 16, :].astype(F32)
        idx = 0 if slot is None else slot + 1
        half = 0.5 * ((tail[0:1] + tail[1:2]) + tail[2:3])
        rowaux[idx, 0:1, :] = half
        rowaux[idx, 1:2, :] = 1.0 / tail[3:4]

    def make(d, q):
        cols = pl.ds(q * cw, cw)
        right = emb[cols, :] if d == 0 else gemb[d - 1, cols, :]
        half_r = rowaux[d, 0:1, cols]
        inv_r = rowaux[d, 1:2, cols]
        for r in range(4):
            rs = pl.ds(r * (rows // 4), rows // 4)
            cross = lax.dot_general(emb[rs, :], right, NT, preferred_element_type=F32)
            t = (cross - (col_aux[rs, 0:1] + half_r)) * (col_aux[rs, 1:2] * inv_r)
            tiles[d, rs, cols] = jnp.exp2(t).astype(BF16)

    def row_product(vec, d, q):
        cols = pl.ds(q * cw, cw)
        return lax.dot_general(vec[:, cols], tiles[d, :, cols], NT, preferred_element_type=F32)

    def part_copy(p, d, q):
        cols = pl.ds(q * cw, cw)
        return remote(
            part.at[p, d - 1, :, cols], got.at[p, d - 1, :, cols],
            psend.at[p, d - 1, q], precv.at[p, d - 1, q], lax.rem(i + d, n),
        )

    def mate_copy(slot, d, q):
        cols = pl.ds(q * cw, cw)
        return remote(
            part.at[1, d - 1, :, cols], mate.at[slot, :, cols],
            msend.at[slot, q], mrecv.at[slot, q], i + 1 - 2 * core,
        )

    def col_product(p, d, q, own_vec):
        cols = pl.ds(q * cw, cw)
        part[p, d - 1, :, cols] = m_ref[d] * lax.dot_general(
            own_vec, tiles[d, :, cols], NN, preferred_element_type=F32
        )
        if p == 0:
            part_copy(p, d, q).start()

    own_v = pack.at[pl.ds(0, k)]
    prepare_aux(None)
    acc[...] = jnp.zeros_like(acc)
    for q in range(CHUNKS):
        make(0, q)
        acc[...] += (2.0 * m_ref[0]) * row_product(own_v, 0, q)

    def arrive(d, q, then):
        @pl.when(i + d < n)
        def _():
            wait_piece(d - 1, q)
            if q == 0:
                prepare_aux(d - 1)
        start(then, q)

    for d, then in ((4, fwd4), (2, fwd2), (3, []), (1, [])):
        arrive(d, 0, then)

    for q in range(CHUNKS):
        arrive(4, q + 1, fwd4)
        arrive(2, q + 1, fwd2)
        for d in (4, 2, 3, 1):
            if d in (3, 1):
                arrive(d, q + 1, [])

            @pl.when(i + d < n)
            def _():
                make(d, q)
                col_product(0, d, q, own_v[...])
                acc[...] += m_ref[d] * row_product(gpack.at[d - 1, pl.ds(0, k)], d, q)

    def arrives(p, d):
        if p == 0 or d in (2, 4):
            return i - d >= 0
        return one if d == 1 else i < 0

    def finish_sum(p):
        for d in (1, 2, 3, 4):
            @pl.when(arrives(p, d))
            def _():
                for q in range(CHUNKS):
                    part_copy(p, d, q).wait_recv()
                acc[...] += got[p, d - 1]

    def factor(p):
        y = acc[...]
        total = lax.dot_general(y, y, NT, precision=HIGH, preferred_element_type=F32)
        total = jnp.concatenate([total[: k // 2], total[k // 2 :]], 1)
        for s, (stride, radix) in enumerate(stages):
            pos = lax.rem(lax.div(i, stride), radix)
            base = i - pos * stride
            gram[p, s, pos] = total
            copies = []
            for t in range(1, radix):
                peer = lax.rem(pos + t, radix)
                copies.append((
                    remote(gram.at[p, s, pos], gram.at[p, s, pos], gsend.at[p, s, t], grecv.at[p, s, pos], base + peer * stride),
                    remote(gram.at[p, s, pos], gram.at[p, s, peer], gsend.at[p, s, t], grecv.at[p, s, peer], base + peer * stride),
                ))
            for c, _ in copies:
                c.start()
            for c, w in copies:
                w.wait_recv()
            total = gram[p, s, 0]
            for t in range(1, radix):
                total = total + gram[p, s, t]
            for c, _ in copies:
                c.wait_send()
        total = jnp.concatenate([total[:, :k], total[:, k:]], 0)
        return lax.dot_general(inverse_factor(total), acc[...], NN, precision=HIGH, preferred_element_type=F32)

    finish_sum(0)
    qown[...] = factor(0).astype(BF16)

    def q_copy(d, dev):
        return remote(qown, gq.at[d - 1], qsend.at[d - 1], qrecv.at[d - 1], dev)

    for d in (4, 3, 2, 1):
        @pl.when(i - d >= 0)
        def _():
            q_copy(d, i - d).start()

    mates = [
        (0, 3, zero & (i + 3 < n)),
        (1, 3, one & (i + 3 < n)),
        (0, 1, one & (i + 1 < n)),
    ]
    for d in (3, 1, 2, 4):
        @pl.when(i + d < n)
        def _():
            for q in range(CHUNKS):
                col_product(1, d, q, qown[...])
        for slot, dist, cond in mates:
            if dist == d:
                @pl.when(cond)
                def _():
                    for q in range(CHUNKS):
                        mate_copy(slot, d, q).start()
        if d == 1:
            @pl.when(zero)
            def _():
                for q in range(CHUNKS):
                    part_copy(1, 1, q).start()
    for d in (4, 2):
        for q in range(CHUNKS):
            cols = pl.ds(q * cw, cw)
            if d == 4:
                @pl.when(zero & (i + 4 < n))
                def _():
                    mate_copy(1, 3, q).wait_recv()
                    part[1, 3, :, cols] += mate[1, :, cols]
            else:
                @pl.when(i + 2 < n)
                def _():
                    mate_copy(0, 1, q).wait_recv()
                    part[1, 1, :, cols] += mate[0, :, cols]

            @pl.when(i + d < n)
            def _():
                part_copy(1, d, q).start()

    acc[...] = jnp.zeros_like(acc)
    for q in range(CHUNKS):
        acc[...] += (2.0 * m_ref[0]) * row_product(qown, 0, q)
    for d in (1, 2, 3, 4):
        @pl.when(i + d < n)
        def _():
            q_copy(d, i).wait_recv()
            for q in range(CHUNKS):
                acc[...] += m_ref[d] * row_product(gq.at[d - 1], d, q)

    finish_sum(1)
    out[...] = out_scale * factor(1)

    for entries in (own_sends, fwd4, fwd2):
        for kind, source, slot, dev, cond in entries:
            @pl.when(cond)
            def _():
                for q in range(CHUNKS + 1):
                    send(kind, q, source, slot, dev).wait_send()
    for d in (1, 2, 3, 4):
        @pl.when(i - d >= 0)
        def _():
            q_copy(d, i).wait_send()

        for p in range(2):
            if p == 0 or d in (2, 4):
                sent = i + d < n
            elif d == 1:
                sent = zero
            else:
                continue

            @pl.when(sent)
            def _():
                for q in range(CHUNKS):
                    part_copy(p, d, q).wait_send()
    for slot, dist, cond in mates:
        @pl.when(cond)
        def _():
            for q in range(CHUNKS):
                mate_copy(slot, dist, q).wait_send()


def local(embeddings, local_scales, start, pairs):
    n = lax.axis_size("blk") * lax.axis_size("sub")
    i = lax.axis_index(("blk", "sub"))
    rows, width = embeddings.shape[1:]
    k = start.shape[2]
    stages = []
    stride = 1
    while stride < n:
        radix = min(4, n // stride)
        stages.append((stride, radix))
        stride *= radix
    ns = len(stages)
    vm = pl.BlockSpec(memory_space=pltpu.VMEM)
    dma = pltpu.SemaphoreType.DMA
    res = pl.pallas_call(
        functools.partial(kernel, n, rows, width, k, tuple(stages), math.sqrt(n * rows)),
        out_shape=jax.ShapeDtypeStruct((k, rows), F32),
        in_specs=[vm, vm, vm, vm],
        out_specs=vm,
        scratch_shapes=[
            pltpu.VMEM((k + 16, rows), BF16),
            pltpu.VMEM((rows, 8), F32),
            pltpu.VMEM((4, rows, width), BF16),
            pltpu.VMEM((4, k + 16, rows), BF16),
            pltpu.VMEM((k, rows), BF16),
            pltpu.VMEM((4, k, rows), BF16),
            pltpu.VMEM((5, rows, rows), BF16),
            pltpu.VMEM((k, rows), F32),
            pltpu.VMEM((2, 4, k, rows), F32),
            pltpu.VMEM((2, 4, k, rows), F32),
            pltpu.VMEM((2, ns, 4, k // 2, 2 * k), F32),
            pltpu.VMEM((5, 8, rows), F32),
            pltpu.VMEM((2, k, rows), F32),
            dma((2, CHUNKS)),
            dma((2, CHUNKS)),
            dma((7, CHUNKS + 1)),
            dma((4, CHUNKS + 1)),
            dma((4,)),
            dma((4,)),
            dma((2, 4, CHUNKS)),
            dma((2, 4, CHUNKS)),
            dma((2, ns, 4)),
            dma((2, ns, 4)),
        ],
        compiler_params=pltpu.CompilerParams(
            collective_id=0, has_side_effects=True, vmem_limit_bytes=56 * 1024 * 1024
        ),
    )(pairs, local_scales, start[0], embeddings[0])
    return res.T[None]


def solution(mesh):
    in_specs = (
        P(("groups", "blk", "sub"), None, None),
        P(("groups", "blk", "sub"), None),
        P(("groups", "blk", "sub"), None, None),
        P("groups", None),
    )
    out_specs = P(("groups", "blk", "sub"), None, None)
    return jax.shard_map(local, mesh=mesh, in_specs=in_specs, out_specs=out_specs, check_vma=False)
```

```python
import functools
import math

import jax
import jax.numpy as jnp
from jax import lax
from jax.experimental import pallas as pl
from jax.experimental.pallas import tpu as pltpu
from jax.sharding import PartitionSpec as P

REACH = 4
CHUNKS = 4
STEP = 2
MESH = pl.DeviceIdType.MESH
HIGH = lax.Precision.HIGHEST
F32 = jnp.float32
BF16 = jnp.bfloat16
NN = (((1,), (0,)), ((), ()))
NT = (((1,), (1,)), ((), ()))


def inverse_factor(gram):
    size = gram.shape[0]
    eye = (
        lax.broadcasted_iota(jnp.int32, (size, size), 0)
        == lax.broadcasted_iota(jnp.int32, (size, size), 1)
    ).astype(F32)
    both = jnp.concatenate([gram, eye], 1)
    groups = [both[8 * g : 8 * g + 8] for g in range(size // 8)]
    below = lax.broadcasted_iota(jnp.int32, (8, 1), 0)
    done = []
    for j in range(0, size, STEP):
        g, r = divmod(j, 8)
        last = size // 8
        line = [groups[g][r + t : r + t + 1] for t in range(STEP)]
        head = [[line[t][:, j + u : j + u + 1] for u in range(STEP)] for t in range(STEP)]
        cols = [[groups[h][:, j + t : j + t + 1] for h in range(g, last)] for t in range(STEP)]
        inv = []
        for t in range(STEP):
            inv.append(1.0 / head[t][t])
            for u in range(t + 1, STEP):
                f = head[t][u] * inv[t]
                line[u] = line[u] - f * line[t]
                cols[u] = [cu - f * ct for cu, ct in zip(cols[u], cols[t])]
                head[u] = [hu - f * ht for hu, ht in zip(head[u], head[t])]
            done.append(line[t] * lax.rsqrt(head[t][t]))
        scaled = [line[t] * inv[t] for t in range(STEP)]
        for h in range(g, last):
            if h == g and r + STEP == 8:
                continue
            update = cols[0][h - g] * scaled[0]
            for t in range(1, STEP):
                update = update + cols[t][h - g] * scaled[t]
            if h == g:
                update = jnp.where(below >= r + STEP, update, 0.0)
            groups[h] = groups[h] - update
    return jnp.concatenate(done, 0)[:, size:]


def kernel(
    n, rows, width, k, stages, out_scale,
    pairs, scales, start_vec, emb, out,
    pack, col_aux,
    gemb, gpack, qown, gq, tiles, acc, part, got, gram, rowaux,
    mate, msend, mrecv, esend, erecv, qsend, qrecv, psend, precv, gsend, grecv,
):
    i = lax.axis_index(("blk", "sub"))
    core = lax.rem(i, 2)
    quad = lax.rem(i, 4)
    cw = rows // CHUNKS

    def to(dev):
        return {"blk": lax.div(dev, 2), "sub": lax.rem(dev, 2)}

    def remote(src, dst, ss, rs, dev):
        return pltpu.make_async_remote_copy(
            src_ref=src, dst_ref=dst, send_sem=ss, recv_sem=rs, device_id=to(dev), device_id_type=MESH
        )

    barrier = pltpu.get_barrier_semaphore()

    @pl.loop(1, n)
    def _(t):
        pl.semaphore_signal(barrier, inc=1, device_id=to(lax.rem(i + t, n)), device_id_type=MESH)

    pl.semaphore_wait(barrier, n - 1)

    def piece(slot, q):
        if q == 0:
            return pack if slot is None else gpack.at[slot]
        sl = pl.ds((q - 1) * cw, cw)
        return emb.at[sl] if slot is None else gemb.at[slot, sl]

    def send(kind, q, source, slot, dev):
        return remote(piece(source, q), piece(slot, q), esend.at[kind, q], erecv.at[slot, q], dev)

    def wait_piece(slot, q):
        remote(piece(slot, q), piece(slot, q), esend.at[0, q], erecv.at[slot, q], i).wait_recv()

    first_quad, later = quad < 2, quad >= 2
    one, zero = core == 1, core == 0
    own_sends = [
        (0, None, 3, i - 4, i >= 4),
        (1, None, 1, i - 2, later),
        (2, None, 0, i - 1, one),
    ]
    fwd4 = [
        (3, 3, 1, i + 2, first_quad & (i + 4 < n)),
        (5, 3, 2, i + 1, zero & (i + 4 < n)),
    ]
    fwd2 = [
        (4, 1, 2, i - 1, one & (i + 2 < n)),
        (6, 1, 0, i + 1, zero & (i + 2 < n)),
    ]

    def start(entries, q):
        for kind, source, slot, dev, cond in entries:
            @pl.when(cond)
            def _():
                send(kind, q, source, slot, dev).start()

    for q in range(1, CHUNKS + 1):
        start(own_sends, q)
        if q > 1:
            continue
        ones = jnp.ones((8, width), BF16)
        squares = []
        for c in range(CHUNKS):
            x = emb[c * cw : (c + 1) * cw, :].astype(F32)
            x = x * x
            big = x.astype(BF16)
            small = (x - big.astype(F32)).astype(BF16)
            squares.append(
                lax.dot_general(ones, big, NT, preferred_element_type=F32)
                + lax.dot_general(ones, small, NT, preferred_element_type=F32)
            )
        sq = jnp.concatenate(squares, 1)
        scale = scales[...].astype(F32)
        high = sq.astype(BF16).astype(F32)
        mid = (sq - high).astype(BF16).astype(F32)
        low = (sq - high) - mid
        line = lax.broadcasted_iota(jnp.int32, (8, rows), 0)
        tail = jnp.where(line == 0, high, jnp.where(line == 1, mid, jnp.where(line == 2, low, scale)))
        pack[k : k + 16, :] = jnp.concatenate([tail, tail], 0).astype(BF16)
        pack[0:k, :] = start_vec[...].astype(F32).T.astype(BF16)
        col_aux[...] = jnp.where(line == 0, 0.5 * sq, (2.0 / math.log(2.0)) / scale).T
        start(own_sends, 0)

    offset = pairs[:, 1:2] - i
    held = pairs[:, 0:1] == i
    m_ref = [
        jnp.sum((held & (offset == d)).astype(F32), 0, keepdims=True) for d in range(REACH + 1)
    ]

    def prepare_aux(slot):
        tail = (pack if slot is None else gpack.at[slot])[k : k + 16, :].astype(F32)
        idx = 0 if slot is None else slot + 1
        half = 0.5 * ((tail[0:1] + tail[1:2]) + tail[2:3])
        rowaux[idx, 0:1, :] = half
        rowaux[idx, 1:2, :] = 1.0 / tail[3:4]

    def make(d, q):
        cols = pl.ds(q * cw, cw)
        right = emb[cols, :] if d == 0 else gemb[d - 1, cols, :]
        half_r = rowaux[d, 0:1, cols]
        inv_r = rowaux[d, 1:2, cols]
        for r in range(4):
            rs = pl.ds(r * (rows // 4), rows // 4)
            cross = lax.dot_general(emb[rs, :], right, NT, preferred_element_type=F32)
            t = (cross - (col_aux[rs, 0:1] + half_r)) * (col_aux[rs, 1:2] * inv_r)
            tiles[d, rs, cols] = jnp.exp2(t).astype(BF16)

    def row_product(vec, d, q):
        cols = pl.ds(q * cw, cw)
        return lax.dot_general(vec[:, cols], tiles[d, :, cols], NT, preferred_element_type=F32)

    def part_copy(p, d, q):
        cols = pl.ds(q * cw, cw)
        return remote(
            part.at[p, d - 1, :, cols], got.at[p, d - 1, :, cols],
            psend.at[p, d - 1, q], precv.at[p, d - 1, q], lax.rem(i + d, n),
        )

    def mate_copy(slot, d, q):
        cols = pl.ds(q * cw, cw)
        return remote(
            part.at[1, d - 1, :, cols], mate.at[slot, :, cols],
            msend.at[slot, q], mrecv.at[slot, q], i + 1 - 2 * core,
        )

    def col_product(p, d, q, own_vec):
        cols = pl.ds(q * cw, cw)
        part[p, d - 1, :, cols] = m_ref[d] * lax.dot_general(
            own_vec, tiles[d, :, cols], NN, preferred_element_type=F32
        )
        if p == 0:
            part_copy(p, d, q).start()

    own_v = pack.at[pl.ds(0, k)]
    prepare_aux(None)
    acc[...] = jnp.zeros_like(acc)
    for q in range(CHUNKS):
        make(0, q)
        acc[...] += (2.0 * m_ref[0]) * row_product(own_v, 0, q)

    def arrive(d, q, then):
        @pl.when(i + d < n)
        def _():
            wait_piece(d - 1, q)
            if q == 0:
                prepare_aux(d - 1)
        start(then, q)

    for d, then in ((4, fwd4), (2, fwd2), (3, []), (1, [])):
        arrive(d, 0, then)

    def work(d, q):
        @pl.when(i + d < n)
        def _():
            make(d, q)
            col_product(0, d, q, own_v[...])
            acc[...] += m_ref[d] * row_product(gpack.at[d - 1, pl.ds(0, k)], d, q)

    for q in range(CHUNKS + 1):
        if q < CHUNKS:
            arrive(4, q + 1, fwd4)
        if q > 0:
            arrive(3, q, [])
            work(3, q - 1)
        if q < CHUNKS:
            arrive(2, q + 1, fwd2)
        if q > 0:
            arrive(1, q, [])
            work(1, q - 1)
        if q < CHUNKS:
            work(4, q)
            work(2, q)

    def arrives(p, d):
        if p == 0 or d in (2, 4):
            return i - d >= 0
        return one if d == 1 else i < 0

    def finish_sum(p):
        for d in (1, 2, 3, 4):
            @pl.when(arrives(p, d))
            def _():
                for q in range(CHUNKS):
                    part_copy(p, d, q).wait_recv()
                acc[...] += got[p, d - 1]

    def factor(p):
        y = acc[...]
        total = lax.dot_general(y, y, NT, precision=HIGH, preferred_element_type=F32)
        total = jnp.concatenate([total[: k // 2], total[k // 2 :]], 1)
        for s, (stride, radix) in enumerate(stages):
            pos = lax.rem(lax.div(i, stride), radix)
            base = i - pos * stride
            gram[p, s, pos] = total
            copies = []
            for t in range(1, radix):
                peer = lax.rem(pos + t, radix)
                copies.append((
                    remote(gram.at[p, s, pos], gram.at[p, s, pos], gsend.at[p, s, t], grecv.at[p, s, pos], base + peer * stride),
                    remote(gram.at[p, s, pos], gram.at[p, s, peer], gsend.at[p, s, t], grecv.at[p, s, peer], base + peer * stride),
                ))
            for c, _ in copies:
                c.start()
            for c, w in copies:
                w.wait_recv()
            total = gram[p, s, 0]
            for t in range(1, radix):
                total = total + gram[p, s, t]
            for c, _ in copies:
                c.wait_send()
        total = jnp.concatenate([total[:, :k], total[:, k:]], 0)
        return lax.dot_general(inverse_factor(total), acc[...], NN, precision=HIGH, preferred_element_type=F32)

    finish_sum(0)
    qown[...] = factor(0).astype(BF16)

    def q_copy(d, dev):
        return remote(qown, gq.at[d - 1], qsend.at[d - 1], qrecv.at[d - 1], dev)

    for d in (4, 3, 2, 1):
        @pl.when(i - d >= 0)
        def _():
            q_copy(d, i - d).start()

    mates = [
        (0, 3, zero & (i + 3 < n)),
        (1, 3, one & (i + 3 < n)),
        (0, 1, one & (i + 1 < n)),
    ]
    for d in (3, 1, 2, 4):
        @pl.when(i + d < n)
        def _():
            part[1, d - 1] = m_ref[d] * lax.dot_general(
                qown[...], tiles[d], NN, preferred_element_type=F32
            )
        for slot, dist, cond in mates:
            if dist == d:
                @pl.when(cond)
                def _():
                    for q in range(CHUNKS):
                        mate_copy(slot, d, q).start()
        if d == 1:
            @pl.when(zero)
            def _():
                for q in range(CHUNKS):
                    part_copy(1, 1, q).start()
    for d in (4, 2):
        for q in range(CHUNKS):
            cols = pl.ds(q * cw, cw)
            if d == 4:
                @pl.when(zero & (i + 4 < n))
                def _():
                    mate_copy(1, 3, q).wait_recv()
                    part[1, 3, :, cols] += mate[1, :, cols]
            else:
                @pl.when(i + 2 < n)
                def _():
                    mate_copy(0, 1, q).wait_recv()
                    part[1, 1, :, cols] += mate[0, :, cols]

            @pl.when(i + d < n)
            def _():
                part_copy(1, d, q).start()

    acc[...] = (2.0 * m_ref[0]) * lax.dot_general(
        qown[...], tiles[0], NT, preferred_element_type=F32
    )
    for d in (1, 2, 3, 4):
        @pl.when(i + d < n)
        def _():
            q_copy(d, i).wait_recv()
            acc[...] += m_ref[d] * lax.dot_general(
                gq[d - 1], tiles[d], NT, preferred_element_type=F32
            )

    finish_sum(1)
    out[...] = out_scale * factor(1)

    for entries in (own_sends, fwd4, fwd2):
        for kind, source, slot, dev, cond in entries:
            @pl.when(cond)
            def _():
                for q in range(CHUNKS + 1):
                    send(kind, q, source, slot, dev).wait_send()
    for d in (1, 2, 3, 4):
        @pl.when(i - d >= 0)
        def _():
            q_copy(d, i).wait_send()

        for p in range(2):
            if p == 0 or d in (2, 4):
                sent = i + d < n
            elif d == 1:
                sent = zero
            else:
                continue

            @pl.when(sent)
            def _():
                for q in range(CHUNKS):
                    part_copy(p, d, q).wait_send()
    for slot, dist, cond in mates:
        @pl.when(cond)
        def _():
            for q in range(CHUNKS):
                mate_copy(slot, dist, q).wait_send()


def local(embeddings, local_scales, start, pairs):
    n = lax.axis_size("blk") * lax.axis_size("sub")
    i = lax.axis_index(("blk", "sub"))
    rows, width = embeddings.shape[1:]
    k = start.shape[2]
    stages = []
    stride = 1
    while stride < n:
        radix = min(4, n // stride)
        stages.append((stride, radix))
        stride *= radix
    ns = len(stages)
    vm = pl.BlockSpec(memory_space=pltpu.VMEM)
    dma = pltpu.SemaphoreType.DMA
    res = pl.pallas_call(
        functools.partial(kernel, n, rows, width, k, tuple(stages), math.sqrt(n * rows)),
        out_shape=jax.ShapeDtypeStruct((k, rows), F32),
        in_specs=[vm, vm, vm, vm],
        out_specs=vm,
        scratch_shapes=[
            pltpu.VMEM((k + 16, rows), BF16),
            pltpu.VMEM((rows, 8), F32),
            pltpu.VMEM((4, rows, width), BF16),
            pltpu.VMEM((4, k + 16, rows), BF16),
            pltpu.VMEM((k, rows), BF16),
            pltpu.VMEM((4, k, rows), BF16),
            pltpu.VMEM((5, rows, rows), BF16),
            pltpu.VMEM((k, rows), F32),
            pltpu.VMEM((2, 4, k, rows), F32),
            pltpu.VMEM((2, 4, k, rows), F32),
            pltpu.VMEM((2, ns, 4, k // 2, 2 * k), F32),
            pltpu.VMEM((5, 8, rows), F32),
            pltpu.VMEM((2, k, rows), F32),
            dma((2, CHUNKS)),
            dma((2, CHUNKS)),
            dma((7, CHUNKS + 1)),
            dma((4, CHUNKS + 1)),
            dma((4,)),
            dma((4,)),
            dma((2, 4, CHUNKS)),
            dma((2, 4, CHUNKS)),
            dma((2, ns, 4)),
            dma((2, ns, 4)),
        ],
        compiler_params=pltpu.CompilerParams(
            collective_id=0, has_side_effects=True, vmem_limit_bytes=56 * 1024 * 1024
        ),
    )(pairs, local_scales, start[0], embeddings[0])
    return res.T[None]


def solution(mesh):
    in_specs = (
        P(("groups", "blk", "sub"), None, None),
        P(("groups", "blk", "sub"), None),
        P(("groups", "blk", "sub"), None, None),
        P("groups", None),
    )
    out_specs = P(("groups", "blk", "sub"), None, None)
    return jax.shard_map(local, mesh=mesh, in_specs=in_specs, out_specs=out_specs, check_vma=False)
```
